32 devices in a mesh: ctx: 16 (over z, x, core), fsdp: 2 (over y).
Axes of the slice: x: 2, y: 2, z: 4, core: 2. Of those that a mesh axis runs over, the one named last changes fastest.
Arguments:
- tokens: bfloat16 [2, 6144, 576], P('fsdp', 'ctx'), may hold values from -6 to 6
- cotangent: bfloat16 [2, 6144, 576], P('fsdp', 'ctx'), may hold values from -6 to 6
- block_place: int32 [32], replicated, may hold values from 0 to 31, as said below
- norm_attn: bfloat16 [576], P('fsdp'), may hold values from 0.5 to 1.5
- w_query: bfloat16 [576, 576], P('fsdp'), may hold values from -0.25 to 0.25
- w_key: bfloat16 [576, 192], P('fsdp'), may hold values from -0.25 to 0.25
- w_value: bfloat16 [576, 192], P('fsdp'), may hold values from -0.25 to 0.25
- w_out: bfloat16 [576, 576], P('fsdp'), may hold values from -6 to 6
- norm_ffn: bfloat16 [576], P('fsdp'), may hold values from 0.5 to 1.5
- w_gate: bfloat16 [576, 1536], P('fsdp'), may hold values from -0.25 to 0.25
- w_up: bfloat16 [576, 1536], P('fsdp'), may hold values from -0.25 to 0.25
- w_down: bfloat16 [1536, 576], P('fsdp'), may hold values from -0.15625 to 0.15625
Outputs:
- layer_out: bfloat16 [2, 6144, 576], P('fsdp', 'ctx')
- grad_tokens: float32 [2, 6144, 576], P('fsdp', 'ctx')
- grad_norm_attn: float32 [576], P('fsdp')
- grad_w_query: float32 [576, 576], P('fsdp')
- grad_w_key: float32 [576, 192], P('fsdp')
- grad_w_value: float32 [576, 192], P('fsdp')
- grad_w_out: float32 [576, 576], P('fsdp')
- grad_norm_ffn: float32 [576], P('fsdp')
- grad_w_gate: float32 [576, 1536], P('fsdp')
- grad_w_up: float32 [576, 1536], P('fsdp')
- grad_w_down: float32 [1536, 576], P('fsdp')
The draws below stay inside these ranges and needn't reach their ends.
Inputs may be any that keep to these rules, and one draw needn't show every extreme that they name: `block_place`: a permutation of the 32 blocks in which stored blocks 2i and 2i + 1 have places that add up to 31.
All inputs are finite; a program needn't handle non-finite values.
Results may differ from the reference program's by a relative error of at most 0.025.
Values may be sent and summed in bfloat16 or wider, within the bound.
A program may use at most 128 MiB of HBM per device.

```python
import jax
import jax.numpy as jnp
from jax import lax

D = 576
HEADS = 9
KV_HEADS = 3
HEAD = 64
FF = 1536
HALF = 192
LENGTH = 6144
BLOCKS = 32
SEQS = 2


def draw_block_place(key, part):
    key = jax.random.fold_in(key, 11)
    pair_key, flip_key = jax.random.split(key)
    pairs = BLOCKS // 2
    early = jax.random.permutation(pair_key, pairs).astype(jnp.int32)
    late = (BLOCKS - 1 - early).astype(jnp.int32)
    flip = jax.random.randint(flip_key, (pairs,), 0, 2).astype(jnp.int32)
    first = early * (1 - flip) + late * flip
    second = late * (1 - flip) + early * flip
    return jnp.stack([first, second], 1).reshape(BLOCKS).astype(jnp.int32)


def block_scale(rng, dims, pieces, least, high):
    level = 1.0
    for dim, shards_of in pieces:
        heights = jax.random.uniform(jax.random.fold_in(jax.random.fold_in(rng, 6), dim), (shards_of,), jnp.float32, least / len(pieces), high / len(pieces))
        level = level * jnp.repeat(jnp.exp(heights), dims[dim] // shards_of).reshape((-1,) + (1,) * (len(dims) - 1 - dim))
    return level


def centred(key, extent, deviation, bound, shards=(), held_as=jnp.bfloat16):
    values = deviation * jax.random.normal(key, extent, jnp.float32)
    if shards:
        values = values * block_scale(key, extent, shards, -0.22, 0.18)
    return jnp.clip(values, -bound, bound).astype(held_as)


def setup_inputs(seed: int = 0) -> dict:
    seeds = jax.random.split(jax.random.key(seed), 13)
    tokens = centred(seeds[0], (SEQS, LENGTH, D), 1.0, 6.0, ((0, 2), (1, 16)))
    cotangent = centred(seeds[1], (SEQS, LENGTH, D), 1.0, 6.0, ((0, 2), (1, 16)))
    block_place = draw_block_place(jax.random.fold_in(seeds[12], 71), 0)
    norm_attn = jnp.clip(1.0 + 0.1 * jax.random.normal(seeds[3], (D,), jnp.float32), 0.5, 1.5).astype(jnp.bfloat16)
    w_query = centred(seeds[4], (D, HEADS * HEAD), D ** -0.5, 0.25, ((0, 2),))
    w_key = centred(seeds[5], (D, KV_HEADS * HEAD), D ** -0.5, 0.25, ((0, 2),))
    w_value = centred(seeds[6], (D, KV_HEADS * HEAD), D ** -0.5, 0.25, ((0, 2),))
    w_out = centred(seeds[7], (HEADS * HEAD, D), 1 ** -0.5, 6.0, ((0, 2),))
    norm_ffn = jnp.clip(1.0 + 0.1 * jax.random.normal(seeds[8], (D,), jnp.float32), 0.5, 1.5).astype(jnp.bfloat16)
    w_gate = centred(seeds[9], (D, FF), D ** -0.5, 0.25, ((0, 2),))
    w_up = centred(seeds[10], (D, FF), D ** -0.5, 0.25, ((0, 2),))
    w_down = centred(seeds[11], (FF, D), FF ** -0.5, 0.15625, ((0, 2),))
    return dict(tokens=tokens, cotangent=cotangent, block_place=block_place, norm_attn=norm_attn, w_query=w_query, w_key=w_key, w_value=w_value, w_out=w_out, norm_ffn=norm_ffn, w_gate=w_gate, w_up=w_up, w_down=w_down)


@jax.custom_vjp
def low(v):
    return lax.optimization_barrier(v.astype(jnp.bfloat16)).astype(jnp.float32)

@jax.custom_vjp
def low_back(v):
    return v

def low_keep(v):
    return (low(v), None)

def low_pass(kept, grad):
    return (grad,)

def back_keep(v):
    return (v, None)

def back_low(kept, grad):
    return (low(grad),)
low.defvjp(low_keep, low_pass)
low_back.defvjp(back_keep, back_low)
HIGH = lax.Precision.HIGHEST
eps_norm = 1e-05
rope_base = 100000.0

def positions_of(block_place):
    rows = jnp.arange(LENGTH, dtype=jnp.int32)
    return (block_place[rows // HALF] * HALF + rows % HALF).astype(jnp.int32)

def rope_tables(positions, width):
    steps = jnp.arange(width // 2, dtype=jnp.float32)
    freq = rope_base ** (-2.0 * steps / width)
    angle = positions.astype(jnp.float32)[:, None] * freq[None, :]
    return (jnp.cos(angle), jnp.sin(angle))

def rotate(v, cosine, sine):
    width = v.shape[-1] // 2
    first, second = (v[..., :width], v[..., width:])
    cosine = cosine[:, None, :]
    sine = sine[:, None, :]
    return jnp.concatenate([first * cosine - second * sine, second * cosine + first * sine], -1)

def normalize(v, gain):
    return v * lax.rsqrt(lax.optimization_barrier(jnp.mean(v * v, -1, keepdims=True)) + eps_norm) * gain

def attend_block(query, qpos, keys, values, kpos):
    raw = jnp.einsum('tgqd,sgd->gqts', query, keys, precision=HIGH) * HEAD ** (-0.5)
    score = low_back(raw)
    allowed = (kpos[None, :] <= qpos[:, None])[None, None]
    score = jnp.where(allowed, score, -1e+30)
    top = lax.optimization_barrier(jnp.max(score, -1, keepdims=True))
    weight = jnp.exp(score - top)
    prob = low(weight / lax.optimization_barrier(jnp.sum(weight, -1, keepdims=True)))
    return jnp.einsum('gqts,sgd->tgqd', prob, values, precision=HIGH)

def layer_one(x, gain_one, wq, wk, wv, wo, gain_two, wg, wu, wd, positions, cosine, sine):
    normed = low(normalize(x, gain_one))
    query = low_back(jnp.dot(normed, wq, precision=HIGH))
    keys = low_back(jnp.dot(normed, wk, precision=HIGH))
    values = low_back(jnp.dot(normed, wv, precision=HIGH))
    query = low(rotate(query.reshape(LENGTH, HEADS, HEAD), cosine, sine))
    keys = low(rotate(keys.reshape(LENGTH, KV_HEADS, HEAD), cosine, sine))
    values = low(values.reshape(LENGTH, KV_HEADS, HEAD))
    qrows = min(512, LENGTH)
    qcount = LENGTH // qrows
    qblocks = query.reshape(qcount, qrows, KV_HEADS, HEADS // KV_HEADS, HEAD)
    pblocks = positions.reshape(qcount, qrows)
    block_fn = jax.checkpoint(lambda pair: attend_block(pair[0], pair[1], keys, values, positions))
    mixed = lax.map(block_fn, (qblocks, pblocks)).reshape(LENGTH, HEADS * HEAD)
    mixed = low(low_back(mixed))
    branch = low_back(jnp.dot(mixed, wo, precision=HIGH))
    middle = x + branch
    normed_two = low(normalize(middle, gain_two))
    gate = low_back(jnp.dot(normed_two, wg, precision=HIGH))
    upper = low_back(jnp.dot(normed_two, wu, precision=HIGH))
    hidden = low(gate * jax.nn.sigmoid(gate) * upper)
    return middle + jnp.dot(hidden, wd, precision=HIGH)

def reference(tokens, cotangent, block_place, norm_attn, w_query, w_key, w_value, w_out, norm_ffn, w_gate, w_up, w_down):
    positions = positions_of(block_place)
    cosine, sine = rope_tables(positions, HEAD)
    floats = [a.astype(jnp.float32) for a in (tokens, norm_attn, w_query, w_key, w_value, w_out, norm_ffn, w_gate, w_up, w_down)]

    def forward(x, *weights):
        return jax.vmap(lambda seq: layer_one(seq, *weights, positions, cosine, sine))(x)
    result, pull = jax.vjp(forward, *floats)
    grads = pull(cotangent.astype(jnp.float32))
    return (result.astype(jnp.bfloat16), grads[0], grads[1], grads[2], grads[3], grads[4], grads[5], grads[6], grads[7], grads[8], grads[9])
```

```python
import jax
import jax.numpy as jnp
from jax import lax
from jax.experimental import pallas as pl
from jax.experimental.pallas import tpu as pltpu
from jax.sharding import PartitionSpec as P

HEADS = 9
KV_HEADS = 3


eps_norm = 1e-05
rope_base = 100000.0


def rotate_t(v, cosine, sine):
    width = v.shape[-2] // 2
    first, second = (v[..., :width, :], v[..., width:, :])
    return jnp.concatenate([first * cosine - second * sine, second * cosine + first * sine], -2)


def normalize(v, gain):
    return v * lax.rsqrt(jnp.mean(v * v, -1, keepdims=True) + eps_norm) * gain


def norm_back(v, gain, grad):
    factor = lax.rsqrt(jnp.mean(v * v, -1, keepdims=True) + eps_norm)
    grad_gain = jnp.sum(grad * v * factor, 0)
    scaled = grad * gain
    grad_in = factor * scaled - v * factor**3 * jnp.mean(scaled * v, -1, keepdims=True)
    return (grad_in, grad_gain)


def inner(left, right):
    return lax.dot_general(
        left, right, (((0,), (0,)), ((), ())), preferred_element_type=jnp.float32
    )


def times_t(left, right):
    return lax.dot_general(
        left, right, (((1,), (1,)), ((), ())), preferred_element_type=jnp.float32
    )


def dot_tn(left, right):
    return lax.dot_general(
        left, right, (((0,), (0,)), ((), ())), preferred_element_type=jnp.float32
    )


def dot_nn(left, right):
    return jnp.dot(left, right, preferred_element_type=jnp.float32)


def causal(half, lanes, full):
    key = lax.broadcasted_iota(jnp.int32, (half, lanes), 0)
    lane = lax.broadcasted_iota(jnp.int32, (half, lanes), 1)
    return (key <= lax.rem(lane, half)) | (lane < full)


def over_blocks(place_ref, width, half, step):
    late, early = place_ref[0], place_ref[1]

    @pl.loop(0, early)
    def both(p):
        step(p, 2 * width, None)

    step(early, 2 * width, causal(half, 2 * width, width))

    @pl.loop(early + 1, late)
    def one(p):
        step(p, width, None)

    step(late, width, causal(half, width, 0))


def attend_kernel(stored_ref, place_ref, qt_ref, kv_ref, out_ref, lse_ref, top_ref, total_ref):
    kv_heads, head, lanes = out_ref.shape
    half = kv_ref.shape[2]
    top_ref[...] = jnp.full_like(top_ref, -1e30)
    total_ref[...] = jnp.zeros_like(total_ref)
    out_ref[...] = jnp.zeros_like(out_ref)

    def step(p, width, allowed):
        j = stored_ref[p]
        for g in range(kv_heads):
            kv = kv_ref[j, g]
            score = dot_nn(kv, qt_ref[g, :, :width])
            if allowed is not None:
                score = jnp.where(allowed, score, -1e30)
            top = top_ref[g, :, :width]
            new_top = jnp.maximum(top, jnp.max(score, 0, keepdims=True))
            weight = jnp.exp(score - new_top)
            fade = jnp.exp(top - new_top)
            top_ref[g, :, :width] = new_top
            total_ref[g, :, :width] = total_ref[g, :, :width] * fade + jnp.sum(
                weight, 0, keepdims=True
            )
            out_ref[g, :, :width] = (
                out_ref[g, :, :width] * fade + dot_tn(kv, weight.astype(jnp.bfloat16))[head:]
            )

    over_blocks(place_ref, lanes // 2, half, step)
    total = total_ref[...]
    lse_ref[...] = top_ref[...] + jnp.log(total)
    out_ref[...] = out_ref[...] / total


def attend_back_kernel(
    stored_ref, place_ref, qt_ref, qn_ref, dot_ref, don_ref, lse_ref, delta_ref, kv_ref,
    dq_ref, dkv_ref,
):
    kv_heads, head, lanes = dq_ref.shape
    half = kv_ref.shape[2]
    dq_ref[...] = jnp.zeros_like(dq_ref)

    def step(p, width, allowed):
        j = stored_ref[p]
        for g in range(kv_heads):
            kv = kv_ref[j, g]
            score = dot_nn(kv, qt_ref[g, :, :width])
            prob = jnp.exp(score - lse_ref[g, :, :width])
            if allowed is not None:
                prob = jnp.where(allowed, prob, 0.0)
            d_prob = dot_nn(kv, dot_ref[g, :, :width])
            d_score = (prob * (d_prob - delta_ref[g, :, :width])).astype(jnp.bfloat16)
            dkv_ref[j, g] = (
                dot_nn(d_score, qn_ref[g, :width]) + dot_nn(prob.astype(jnp.bfloat16), don_ref[g, :width])
            ).astype(jnp.bfloat16)
            dq_ref[g, :, :width] += dot_tn(kv, d_score)[:head]

    over_blocks(place_ref, lanes // 2, half, step)

    @pl.loop(place_ref[0] + 1, dkv_ref.shape[0])
    def unseen(p):
        dkv_ref[stored_ref[p]] = jnp.zeros(dkv_ref.shape[1:], dkv_ref.dtype)


def in_vmem(count):
    return [pl.BlockSpec(memory_space=pltpu.VMEM)] * count


def attend(stored, place, qt, kv):
    kv_heads, wide, lanes = qt.shape
    head = wide // 2
    work = kv.shape[0] * kv_heads * kv.shape[2] * lanes // 2
    return pl.pallas_call(
        attend_kernel,
        out_shape=(
            jax.ShapeDtypeStruct((kv_heads, head, lanes), jnp.float32),
            jax.ShapeDtypeStruct((kv_heads, 1, lanes), jnp.float32),
        ),
        in_specs=[pl.BlockSpec(memory_space=pltpu.SMEM)] * 2 + in_vmem(2),
        out_specs=tuple(in_vmem(2)),
        scratch_shapes=[pltpu.VMEM((kv_heads, 1, lanes), jnp.float32)] * 2,
        compiler_params=pltpu.CompilerParams(vmem_limit_bytes=48 << 20),
        cost_estimate=pl.CostEstimate(
            flops=4 * wide * work, bytes_accessed=2 * kv.size, transcendentals=work
        ),
        name="attend",
    )(stored, place, qt, kv)


def attend_back(stored, place, qt, qn, d_ot, d_on, lse, delta, kv):
    kv_heads, wide, lanes = qt.shape
    head = wide // 2
    work = kv.shape[0] * kv_heads * kv.shape[2] * lanes // 2
    return pl.pallas_call(
        attend_back_kernel,
        out_shape=(
            jax.ShapeDtypeStruct((kv_heads, head, lanes), jnp.float32),
            jax.ShapeDtypeStruct(kv.shape, jnp.bfloat16),
        ),
        in_specs=[pl.BlockSpec(memory_space=pltpu.SMEM)] * 2 + in_vmem(7),
        out_specs=tuple(in_vmem(2)),
        compiler_params=pltpu.CompilerParams(vmem_limit_bytes=48 << 20),
        cost_estimate=pl.CostEstimate(
            flops=10 * wide * work, bytes_accessed=4 * kv.size, transcendentals=work
        ),
        name="attend_back",
    )(stored, place, qt, qn, d_ot, d_on, lse, delta, kv)


def body(
    tokens,
    cotangent,
    block_place,
    norm_attn,
    w_query,
    w_key,
    w_value,
    w_out,
    norm_ffn,
    w_gate,
    w_up,
    w_down,
):
    here = lax.axis_index("ctx")
    tok = tokens.shape[1]
    half = tok // 2
    blocks = block_place.shape[0]
    groups = HEADS // KV_HEADS
    head = w_query.shape[1] // HEADS
    q_width = HEADS * head
    kv_width = KV_HEADS * head
    scale = head ** (-0.5)
    ff = w_gate.shape[1]

    mine = lax.dynamic_slice_in_dim(block_place, 2 * here, 2)
    swap = mine[0] < mine[1]
    place = jnp.where(swap, mine[::-1], mine)
    order = jnp.arange(blocks, dtype=jnp.int32)
    at = jnp.sum(jnp.where(block_place[None, :] == order[:, None], order[None, :], 0), 1)
    stored = (at // 2 * 2 + (order < blocks // 2)).astype(jnp.int32)

    def arrange(rows):
        return jnp.where(swap, jnp.concatenate([rows[half:], rows[:half]], 0), rows)

    first_pack = jnp.concatenate(
        [w_query, w_key, w_value, norm_attn[:, None], norm_ffn[:, None]], 1
    )
    first_pack = lax.all_gather(first_pack, "fsdp", axis=0, tiled=True)
    w_qkv = first_pack[:, : q_width + 2 * kv_width]
    gain_one = first_pack[:, -2].astype(jnp.float32)
    gain_two = first_pack[:, -1].astype(jnp.float32)

    x_rows = arrange(tokens[0]).astype(jnp.float32)
    seed_grad = arrange(cotangent[0])
    positions = (place[:, None] * half + jnp.arange(half, dtype=jnp.int32)[None, :]).reshape(tok)
    freq = rope_base ** (-2.0 * jnp.arange(head // 2, dtype=jnp.float32) / head)
    angle = freq[:, None] * positions.astype(jnp.float32)[None, :]
    cosine, sine = jnp.cos(angle), jnp.sin(angle)

    normed = normalize(x_rows, gain_one).astype(jnp.bfloat16)
    qkv_t = lax.dot_general(
        w_qkv, normed, (((0,), (1,)), ((), ())), preferred_element_type=jnp.float32
    )
    query = rotate_t(qkv_t[:q_width].reshape(HEADS, head, tok), cosine, sine).astype(jnp.bfloat16)
    keys = rotate_t(
        qkv_t[q_width : q_width + kv_width].reshape(KV_HEADS, head, tok), cosine, sine
    ).astype(jnp.bfloat16)
    values = qkv_t[q_width + kv_width :].reshape(KV_HEADS, head, tok).astype(jnp.bfloat16)
    kv = jnp.concatenate([keys, values], 1).reshape(KV_HEADS, 2 * head, 2, half)
    kv = lax.all_gather(jnp.transpose(kv, (2, 0, 3, 1)), "ctx", axis=0, tiled=True)

    def to_lanes(v):
        v = v.reshape(KV_HEADS, groups, head, 2, half)
        return jnp.transpose(v, (0, 2, 3, 1, 4)).reshape(KV_HEADS, head, 2 * groups * half)

    def from_lanes(v):
        v = v.reshape(KV_HEADS, head, 2, groups, half)
        return jnp.transpose(v, (0, 3, 1, 2, 4)).reshape(HEADS, head, tok)

    qt = to_lanes(query * jnp.bfloat16(scale))
    qt = jnp.concatenate([qt, jnp.zeros_like(qt)], 1)
    qn = jnp.swapaxes(qt, 1, 2)
    attn, lse = attend(stored, place, qt, kv)

    wo = lax.all_gather(w_out, "fsdp", axis=0, tiled=True)
    w_ff = lax.all_gather(jnp.concatenate([w_gate, w_up], 1), "fsdp", axis=0, tiled=True)
    wd = lax.all_gather(w_down, "fsdp", axis=0, tiled=True)

    mixed = jnp.transpose(from_lanes(attn.astype(jnp.bfloat16)).reshape(q_width, tok))
    middle = x_rows + dot_nn(mixed, wo)
    normed_two = normalize(middle, gain_two).astype(jnp.bfloat16)
    gate_up = dot_nn(normed_two, w_ff)
    gate, upper = gate_up[:, :ff], gate_up[:, ff:]
    sig = jax.nn.sigmoid(gate)
    hidden = (gate * sig * upper).astype(jnp.bfloat16)
    result = middle + dot_nn(hidden, wd)
    d_hidden = times_t(seed_grad, wd)
    grad_wd = inner(hidden, seed_grad).astype(jnp.bfloat16)
    d_gate = (d_hidden * upper * sig * (1.0 + gate * (1.0 - sig))).astype(jnp.bfloat16)
    d_up = (d_hidden * gate * sig).astype(jnp.bfloat16)
    d_ff = jnp.concatenate([d_gate, d_up], 1)
    grad_ff = inner(normed_two, d_ff).astype(jnp.bfloat16)
    d_norm_two = times_t(d_ff, w_ff)
    d_middle, grad_gain_two = norm_back(middle, gain_two, d_norm_two)
    d_middle = d_middle + seed_grad.astype(jnp.float32)
    d_branch = d_middle.astype(jnp.bfloat16)
    grad_wo = inner(mixed, d_branch).astype(jnp.bfloat16)
    d_mixed_t = times_t(wo, d_branch).astype(jnp.bfloat16)
    d_ot = to_lanes(d_mixed_t)
    delta = jnp.sum(d_ot.astype(jnp.float32) * attn, 1, keepdims=True)
    d_ot = jnp.concatenate([jnp.zeros_like(d_ot), d_ot], 1)
    d_on = jnp.swapaxes(d_ot, 1, 2)

    early = reduce_early(grad_wd, grad_ff, grad_wo)

    dqt, dkv = attend_back(stored, place, qt, qn, d_ot, d_on, lse, delta, kv)
    dkv = lax.psum_scatter(dkv, "ctx", scatter_dimension=0, tiled=True)
    dkv = jnp.transpose(dkv, (1, 3, 0, 2)).reshape(KV_HEADS, 2 * head, tok)
    dk_t = dkv[:, :head].astype(jnp.float32)
    dq_t = from_lanes(dqt) * scale
    d_qkv_t = jnp.concatenate(
        [
            rotate_t(dq_t, cosine, -sine).astype(jnp.bfloat16).reshape(q_width, tok),
            rotate_t(dk_t, cosine, -sine).astype(jnp.bfloat16).reshape(kv_width, tok),
            dkv[:, head:].reshape(kv_width, tok),
        ],
        0,
    )
    grad_qkv = jnp.transpose(dot_nn(d_qkv_t, normed)).astype(jnp.bfloat16)
    d_norm_one = lax.dot_general(
        d_qkv_t, w_qkv, (((0,), (1,)), ((), ())), preferred_element_type=jnp.float32
    )
    d_input, grad_gain_one = norm_back(x_rows, gain_one, d_norm_one)
    grad_input = d_input + d_middle
    late = reduce_late(grad_qkv, grad_gain_one, grad_gain_two)

    grad_wd, grad_ff, grad_wo = early
    grad_qkv, grad_gain_one, grad_gain_two = late
    return (
        arrange(result.astype(jnp.bfloat16))[None],
        arrange(grad_input)[None],
        grad_gain_one,
        grad_qkv[:, :q_width],
        grad_qkv[:, q_width : q_width + kv_width],
        grad_qkv[:, q_width + kv_width :],
        grad_wo,
        grad_gain_two,
        grad_ff[:, :ff],
        grad_ff[:, ff:],
        grad_wd,
    )


def reduce_early(grad_wd, grad_ff, grad_wo):
    def total(v):
        v = lax.psum_scatter(v, "fsdp", scatter_dimension=0, tiled=True)
        return lax.psum(v, "ctx").astype(jnp.float32)

    return total(grad_wd), total(grad_ff), total(grad_wo)


def reduce_late(grad_qkv, grad_gain_one, grad_gain_two):
    gains = jnp.stack([grad_gain_one, grad_gain_two], 1).astype(jnp.bfloat16)
    pack = jnp.concatenate([grad_qkv, gains], 1)
    pack = lax.psum_scatter(pack, "fsdp", scatter_dimension=0, tiled=True)
    pack = lax.psum(pack, "ctx").astype(jnp.float32)
    return pack[:, :-2], pack[:, -2], pack[:, -1]


def solution(mesh):
    placed = (
        P("fsdp", "ctx", None),
        P("fsdp", "ctx", None),
        P(),
        P("fsdp"),
        P("fsdp", None),
        P("fsdp", None),
        P("fsdp", None),
        P("fsdp", None),
        P("fsdp"),
        P("fsdp", None),
        P("fsdp", None),
        P("fsdp", None),
    )
    return jax.shard_map(
        body,
        mesh=mesh,
        in_specs=placed,
        out_specs=(
            P("fsdp", "ctx", None),
            P("fsdp", "ctx", None),
            P("fsdp"),
            P("fsdp", None),
            P("fsdp", None),
            P("fsdp", None),
            P("fsdp", None),
            P("fsdp"),
            P("fsdp", None),
            P("fsdp", None),
            P("fsdp", None),
        ),
        check_vma=False,
    )
```

```python
import functools

import jax
import jax.numpy as jnp
import numpy as np
from jax import lax
from jax.experimental import pallas as pl
from jax.experimental.pallas import tpu as pltpu
from jax.sharding import PartitionSpec as P

HEADS = 9
KV_HEADS = 3


eps_norm = 1e-05
rope_base = 100000.0


def rotate_t(v, cosine, sine):
    width = v.shape[-2] // 2
    first, second = (v[..., :width, :], v[..., width:, :])
    return jnp.concatenate([first * cosine - second * sine, second * cosine + first * sine], -2)


def normalize(v, gain):
    return v * lax.rsqrt(jnp.mean(v * v, -1, keepdims=True) + eps_norm) * gain


def norm_back(v, gain, grad):
    factor = lax.rsqrt(jnp.mean(v * v, -1, keepdims=True) + eps_norm)
    grad_gain = jnp.sum(grad * v * factor, 0)
    scaled = grad * gain
    grad_in = factor * scaled - v * factor**3 * jnp.mean(scaled * v, -1, keepdims=True)
    return (grad_in, grad_gain)


def inner(left, right):
    return lax.dot_general(
        left, right, (((0,), (0,)), ((), ())), preferred_element_type=jnp.float32
    )


def times_t(left, right):
    return lax.dot_general(
        left, right, (((1,), (1,)), ((), ())), preferred_element_type=jnp.float32
    )


def dot_tn(left, right):
    return lax.dot_general(
        left, right, (((0,), (0,)), ((), ())), preferred_element_type=jnp.float32
    )


def dot_nn(left, right):
    return jnp.dot(left, right, preferred_element_type=jnp.float32)


def causal(half, lanes, full):
    key = lax.broadcasted_iota(jnp.int32, (half, lanes), 0)
    lane = lax.broadcasted_iota(jnp.int32, (half, lanes), 1)
    return (key <= lax.rem(lane, half)) | (lane < full)


def over_blocks(place_ref, width, half, step):
    late, early = place_ref[0], place_ref[1]

    @pl.loop(0, early)
    def both(p):
        step(p, 2 * width, None)

    step(early, 2 * width, causal(half, 2 * width, width))

    @pl.loop(early + 1, late)
    def one(p):
        step(p, width, None)

    step(late, width, causal(half, width, 0))


def attend_kernel(stored_ref, place_ref, qt_ref, kv_ref, out_ref, lse_ref, top_ref, total_ref):
    kv_heads, head, lanes = out_ref.shape
    half = kv_ref.shape[2]
    top_ref[...] = jnp.full_like(top_ref, -1e30)
    total_ref[...] = jnp.zeros_like(total_ref)
    out_ref[...] = jnp.zeros_like(out_ref)

    def step(p, width, allowed):
        j = stored_ref[p]
        for g in range(kv_heads):
            kv = kv_ref[j, g]
            score = dot_nn(kv, qt_ref[g, :, :width])
            if allowed is not None:
                score = jnp.where(allowed, score, -1e30)
            top = top_ref[g, :, :width]
            new_top = jnp.maximum(top, jnp.max(score, 0, keepdims=True))
            weight = jnp.exp(score - new_top)
            fade = jnp.exp(top - new_top)
            top_ref[g, :, :width] = new_top
            total_ref[g, :, :width] = total_ref[g, :, :width] * fade + jnp.sum(
                weight, 0, keepdims=True
            )
            out_ref[g, :, :width] = (
                out_ref[g, :, :width] * fade + dot_tn(kv, weight.astype(jnp.bfloat16))[head:]
            )

    over_blocks(place_ref, lanes // 2, half, step)
    total = total_ref[...]
    lse_ref[...] = top_ref[...] + jnp.log(total)
    out_ref[...] = out_ref[...] / total


def attend_back_kernel(
    stored_ref, place_ref, qt_ref, qn_ref, dot_ref, don_ref, lse_ref, delta_ref, kv_ref,
    dq_ref, dkv_ref,
):
    kv_heads, head, lanes = dq_ref.shape
    half = kv_ref.shape[2]
    dq_ref[...] = jnp.zeros_like(dq_ref)

    def step(p, width, allowed):
        j = stored_ref[p]
        for g in range(kv_heads):
            kv = kv_ref[j, g]
            score = dot_nn(kv, qt_ref[g, :, :width])
            prob = jnp.exp(score - lse_ref[g, :, :width])
            if allowed is not None:
                prob = jnp.where(allowed, prob, 0.0)
            d_prob = dot_nn(kv, dot_ref[g, :, :width])
            d_score = (prob * (d_prob - delta_ref[g, :, :width])).astype(jnp.bfloat16)
            dkv_ref[j, g] = (
                dot_nn(d_score, qn_ref[g, :width]) + dot_nn(prob.astype(jnp.bfloat16), don_ref[g, :width])
            ).astype(jnp.bfloat16)
            dq_ref[g, :, :width] += dot_tn(kv, d_score)[:head]

    over_blocks(place_ref, lanes // 2, half, step)

    @pl.loop(place_ref[0] + 1, dkv_ref.shape[0])
    def unseen(p):
        dkv_ref[stored_ref[p]] = jnp.zeros(dkv_ref.shape[1:], dkv_ref.dtype)


def in_vmem(count):
    return [pl.BlockSpec(memory_space=pltpu.VMEM)] * count


def attend(stored, place, qt, kv):
    kv_heads, wide, lanes = qt.shape
    head = wide // 2
    work = kv.shape[0] * kv_heads * kv.shape[2] * lanes // 2
    return pl.pallas_call(
        attend_kernel,
        out_shape=(
            jax.ShapeDtypeStruct((kv_heads, head, lanes), jnp.float32),
            jax.ShapeDtypeStruct((kv_heads, 1, lanes), jnp.float32),
        ),
        in_specs=[pl.BlockSpec(memory_space=pltpu.SMEM)] * 2 + in_vmem(2),
        out_specs=tuple(in_vmem(2)),
        scratch_shapes=[pltpu.VMEM((kv_heads, 1, lanes), jnp.float32)] * 2,
        compiler_params=pltpu.CompilerParams(vmem_limit_bytes=48 << 20),
        cost_estimate=pl.CostEstimate(
            flops=4 * wide * work, bytes_accessed=2 * kv.size, transcendentals=work
        ),
        name="attend",
    )(stored, place, qt, kv)


def attend_back(stored, place, qt, qn, d_ot, d_on, lse, delta, kv):
    kv_heads, wide, lanes = qt.shape
    head = wide // 2
    work = kv.shape[0] * kv_heads * kv.shape[2] * lanes // 2
    return pl.pallas_call(
        attend_back_kernel,
        out_shape=(
            jax.ShapeDtypeStruct((kv_heads, head, lanes), jnp.float32),
            jax.ShapeDtypeStruct(kv.shape, jnp.bfloat16),
        ),
        in_specs=[pl.BlockSpec(memory_space=pltpu.SMEM)] * 2 + in_vmem(7),
        out_specs=tuple(in_vmem(2)),
        compiler_params=pltpu.CompilerParams(vmem_limit_bytes=48 << 20),
        cost_estimate=pl.CostEstimate(
            flops=10 * wide * work, bytes_accessed=4 * kv.size, transcendentals=work
        ),
        name="attend_back",
    )(stored, place, qt, qn, d_ot, d_on, lse, delta, kv)


def flip_bits(order):
    me, row = lax.axis_index("ctx"), lax.axis_index("fsdp")
    found = {}
    for name in order:
        if name == "y":
            found[name] = (row, {"fsdp": 1 - row})
        else:
            step = 1 << CTX_BITS.index(name)
            bit = lax.rem(lax.div(me, step), 2)
            found[name] = (bit, {"ctx": me + step - 2 * step * bit})
    return found


CTX_BITS = ("core", "x", "near", "far")


def at_axis(ref, axis, index):
    return ref.at[(slice(None),) * axis + (index,)]


def tiles(shape):
    return list(np.ndindex(*shape[:-2]))


def reduce_kernel(jobs, *refs):
    count = len(jobs)
    sources, outs = refs[:count], refs[count : 2 * count]
    rest = list(refs[2 * count :])
    landing = [[rest.pop(0) for _ in order] for _, order, _ in jobs]
    send, recv = rest
    bits = flip_bits([n for n in ("y",) + CTX_BITS if any(n in axes for axes, _, _ in jobs)])
    barrier = pltpu.get_barrier_semaphore()
    for _, partner in bits.values():
        pl.semaphore_signal(barrier, inc=1, device_id=partner, device_id_type=pl.DeviceIdType.MESH)
    pl.semaphore_wait(barrier, len(bits))
    used = 0

    def copy(src, dst, name):
        nonlocal used
        made = pltpu.make_async_remote_copy(
            src_ref=src,
            dst_ref=dst,
            send_sem=send.at[used],
            recv_sem=recv.at[used],
            device_id=bits[name][1],
            device_id_type=pl.DeviceIdType.MESH,
        )
        used += 1
        made.start()
        return made

    state = [[source, list(axes), None] for source, (axes, _, _) in zip(sources, jobs)]
    gathers = [list(reversed([n for n in order if n != "y"])) if g else [] for _, order, g in jobs]
    longest = max(len(order) + len(back) for (_, order, _), back in zip(jobs, gathers))

    def begin(i, stage):
        current, axes, _ = state[i]
        order = jobs[i][1]
        if stage < len(order):
            name = order[stage]
            k = axes.index(name)
            away = at_axis(current, k, 1 - bits[name][0])
            state[i][2] = copy(away, landing[i][stage], name)
        elif stage < len(order) + len(gathers[i]):
            name = gathers[i][stage - len(order)]
            done = gathers[i][: stage - len(order)]
            place = tuple(
                slice(None) if n in done else bits[n][0] for n in jobs[i][0] if n != "y"
            )
            part = outs[i].at[place]
            state[i][2] = copy(part, part, name)

    def finish(i, stage):
        current, axes, made = state[i]
        order = jobs[i][1]
        if stage < len(order):
            made.wait()
            name = order[stage]
            k = axes.index(name)
            got = landing[i][stage]
            last = stage == len(order) - 1
            for t in tiles(got.shape):
                mine = current[t[:k] + (bits[name][0],) + t[k:]]
                total = (mine.astype(jnp.float32) + got[t].astype(jnp.float32)).astype(got.dtype)
                if not last:
                    got[t] = total
                elif gathers[i]:
                    outs[i][tuple(bits[n][0] for n in jobs[i][0] if n != "y")] = total
                else:
                    outs[i][...] = total
            state[i][0], state[i][1] = got, axes[:k] + axes[k + 1 :]
        elif stage < len(order) + len(gathers[i]):
            made.wait()

    for i in range(count):
        begin(i, 0)
    for stage in range(longest):
        for i in range(count):
            finish(i, stage)
            begin(i, stage + 1)


def reduce_over(arrays, jobs, name, collective_id):
    outs, scratch, steps = [], [], 0
    for array, (axes, order, gather) in zip(arrays, jobs):
        tile = array.shape[-2:]
        lead = (2,) * (len(axes) - ("y" in axes)) if gather else ()
        outs.append(jax.ShapeDtypeStruct(lead + tile, array.dtype))
        scratch += [
            pltpu.VMEM((2,) * (len(axes) - 1 - s) + tile, array.dtype) for s in range(len(order))
        ]
        steps += len(order) + (len(order) - ("y" in axes) if gather else 0)
    return pl.pallas_call(
        functools.partial(reduce_kernel, jobs),
        out_shape=tuple(outs),
        in_specs=in_vmem(len(arrays)),
        out_specs=tuple(in_vmem(len(arrays))),
        scratch_shapes=scratch + [pltpu.SemaphoreType.DMA((steps,))] * 2,
        compiler_params=pltpu.CompilerParams(
            vmem_limit_bytes=52 << 20, collective_id=collective_id, has_side_effects=True
        ),
        cost_estimate=pl.CostEstimate(
            flops=sum(a.size for a in arrays),
            bytes_accessed=sum(4 * a.size for a in arrays),
            transcendentals=0,
        ),
        name=name,
    )(*arrays)


CTX_AXES = ("far", "near", "x", "core")


def reduce_main(dkv, grad_wd, grad_ff):
    bits = (2,) * 4
    width = grad_ff.shape[1]
    dkv_in = dkv.reshape(bits + (-1, dkv.shape[-1]))
    wd_in = grad_wd.reshape((2,) + bits + (-1, grad_wd.shape[1]))
    rows = grad_ff.shape[0] // 4
    ff_in = grad_ff.reshape(2, 2, rows, 8, width // 8)
    ff_in = jnp.transpose(ff_in, (0, 1, 3, 2, 4)).reshape((2,) + bits + (rows, width // 8))
    half = dkv_in.shape[-2] // 2
    jobs = (
        (CTX_AXES, ("core", "x", "near", "far"), False),
        (CTX_AXES, ("core", "near", "far", "x"), False),
        (("y",) + CTX_AXES, ("core", "y", "x", "near", "far"), True),
        (("y",) + CTX_AXES, ("core", "y", "near", "far", "x"), True),
    )
    one, two, ff, wd = reduce_over(
        (dkv_in[..., :half, :], dkv_in[..., half:, :], ff_in, wd_in), jobs, "reduce_main", 1
    )
    mine = jnp.concatenate([one, two], 0).reshape((2,) + dkv.shape[1:])
    ff = jnp.transpose(ff.reshape(2, 8, rows, width // 8), (0, 2, 1, 3)).reshape(2 * rows, width)
    return mine, ff.astype(jnp.float32), wd.reshape(-1, wd.shape[-1]).astype(jnp.float32)


def reduce_rest(grad_wo, grad_qkv, grad_gain_one, grad_gain_two):
    bits = (2,) * 4
    width = grad_wo.shape[1] + grad_qkv.shape[1]
    rows = grad_wo.shape[0] // 2
    block = -(-(rows + 2) // 64) * 16
    pack = jnp.concatenate([grad_wo, grad_qkv], 1).reshape(2, rows, width)
    gains = jnp.stack([grad_gain_one, grad_gain_two]).astype(pack.dtype).reshape(2, 2, rows)
    gains = jnp.pad(
        jnp.swapaxes(gains, 0, 1), ((0, 0), (0, 4 * block - rows - 2), (0, width - rows))
    )
    pack = jnp.concatenate([pack, gains], 1).reshape(2, 4, block, 4, width // 4)
    pack = jnp.transpose(pack, (0, 1, 3, 2, 4)).reshape((2,) + bits + (block, width // 4))
    jobs = ((("y",) + CTX_AXES, ("core", "y", "x", "near", "far"), True),)
    (pack,) = reduce_over((pack,), jobs, "reduce_rest", 2)
    pack = jnp.transpose(pack.reshape(4, 4, block, width // 4), (0, 2, 1, 3))
    pack = pack.reshape(4 * block, width).astype(jnp.float32)
    cut = grad_wo.shape[1]
    return pack[:rows, :cut], pack[:rows, cut:], pack[rows, :rows], pack[rows + 1, :rows]


def body(
    tokens,
    cotangent,
    block_place,
    norm_attn,
    w_query,
    w_key,
    w_value,
    w_out,
    norm_ffn,
    w_gate,
    w_up,
    w_down,
):
    here = lax.axis_index("ctx")
    tok = tokens.shape[1]
    half = tok // 2
    blocks = block_place.shape[0]
    groups = HEADS // KV_HEADS
    head = w_query.shape[1] // HEADS
    q_width = HEADS * head
    kv_width = KV_HEADS * head
    scale = head ** (-0.5)
    ff = w_gate.shape[1]

    mine = lax.dynamic_slice_in_dim(block_place, 2 * here, 2)
    swap = mine[0] < mine[1]
    place = jnp.where(swap, mine[::-1], mine)
    order = jnp.arange(blocks, dtype=jnp.int32)
    at = jnp.sum(jnp.where(block_place[None, :] == order[:, None], order[None, :], 0), 1)
    stored = (at // 2 * 2 + (order < blocks // 2)).astype(jnp.int32)

    def arrange(rows):
        return jnp.where(swap, jnp.concatenate([rows[half:], rows[:half]], 0), rows)

    first_pack = jnp.concatenate(
        [w_query, w_key, w_value, norm_attn[:, None], norm_ffn[:, None]], 1
    )
    first_pack = lax.all_gather(first_pack, "fsdp", axis=0, tiled=True)
    w_qkv = first_pack[:, : q_width + 2 * kv_width]
    gain_one = first_pack[:, -2].astype(jnp.float32)
    gain_two = first_pack[:, -1].astype(jnp.float32)

    x_rows = arrange(tokens[0]).astype(jnp.float32)
    seed_grad = arrange(cotangent[0])
    positions = (place[:, None] * half + jnp.arange(half, dtype=jnp.int32)[None, :]).reshape(tok)
    freq = rope_base ** (-2.0 * jnp.arange(head // 2, dtype=jnp.float32) / head)
    angle = freq[:, None] * positions.astype(jnp.float32)[None, :]
    cosine, sine = jnp.cos(angle), jnp.sin(angle)

    normed = normalize(x_rows, gain_one).astype(jnp.bfloat16)
    qkv_t = lax.dot_general(
        w_qkv, normed, (((0,), (1,)), ((), ())), preferred_element_type=jnp.float32
    )
    query = rotate_t(qkv_t[:q_width].reshape(HEADS, head, tok), cosine, sine).astype(jnp.bfloat16)
    keys = rotate_t(
        qkv_t[q_width : q_width + kv_width].reshape(KV_HEADS, head, tok), cosine, sine
    ).astype(jnp.bfloat16)
    values = qkv_t[q_width + kv_width :].reshape(KV_HEADS, head, tok).astype(jnp.bfloat16)
    kv = jnp.concatenate([keys, values], 1).reshape(KV_HEADS, 2 * head, 2, half)
    kv = lax.all_gather(jnp.transpose(kv, (2, 0, 3, 1)), "ctx", axis=0, tiled=True)

    def to_lanes(v):
        v = v.reshape(KV_HEADS, groups, head, 2, half)
        return jnp.transpose(v, (0, 2, 3, 1, 4)).reshape(KV_HEADS, head, 2 * groups * half)

    def from_lanes(v):
        v = v.reshape(KV_HEADS, head, 2, groups, half)
        return jnp.transpose(v, (0, 3, 1, 2, 4)).reshape(HEADS, head, tok)

    qt = to_lanes(query * jnp.bfloat16(scale))
    qt = jnp.concatenate([qt, jnp.zeros_like(qt)], 1)
    qn = jnp.swapaxes(qt, 1, 2)
    attn, lse = attend(stored, place, qt, kv)

    wo = lax.all_gather(w_out, "fsdp", axis=0, tiled=True)
    w_ff = lax.all_gather(jnp.concatenate([w_gate, w_up], 1), "fsdp", axis=0, tiled=True)
    wd = lax.all_gather(w_down, "fsdp", axis=0, tiled=True)

    mixed = jnp.transpose(from_lanes(attn.astype(jnp.bfloat16)).reshape(q_width, tok))
    middle = x_rows + dot_nn(mixed, wo)
    normed_two = normalize(middle, gain_two).astype(jnp.bfloat16)
    gate_up = dot_nn(normed_two, w_ff)
    gate, upper = gate_up[:, :ff], gate_up[:, ff:]
    sig = jax.nn.sigmoid(gate)
    hidden = (gate * sig * upper).astype(jnp.bfloat16)
    result = middle + dot_nn(hidden, wd)
    d_hidden = times_t(seed_grad, wd)
    grad_wd = inner(hidden, seed_grad).astype(jnp.bfloat16)
    d_gate = (d_hidden * upper * sig * (1.0 + gate * (1.0 - sig))).astype(jnp.bfloat16)
    d_up = (d_hidden * gate * sig).astype(jnp.bfloat16)
    d_ff = jnp.concatenate([d_gate, d_up], 1)
    grad_ff = inner(normed_two, d_ff).astype(jnp.bfloat16)
    d_norm_two = times_t(d_ff, w_ff)
    d_middle, grad_gain_two = norm_back(middle, gain_two, d_norm_two)
    d_middle = d_middle + seed_grad.astype(jnp.float32)
    d_branch = d_middle.astype(jnp.bfloat16)
    grad_wo = inner(mixed, d_branch).astype(jnp.bfloat16)
    d_mixed_t = times_t(wo, d_branch).astype(jnp.bfloat16)
    d_ot = to_lanes(d_mixed_t)
    delta = jnp.sum(d_ot.astype(jnp.float32) * attn, 1, keepdims=True)
    d_ot = jnp.concatenate([jnp.zeros_like(d_ot), d_ot], 1)
    d_on = jnp.swapaxes(d_ot, 1, 2)

    dqt, dkv = attend_back(stored, place, qt, qn, d_ot, d_on, lse, delta, kv)
    by_halves = lax.axis_size("ctx") == 16 and lax.axis_size("fsdp") == 2
    if by_halves:
        dkv, grad_ff, grad_wd = reduce_main(dkv, grad_wd, grad_ff)
    else:
        grad_wd, grad_ff, grad_wo = reduce_early(grad_wd, grad_ff, grad_wo)
        dkv = lax.psum_scatter(dkv, "ctx", scatter_dimension=0, tiled=True)
    dkv = jnp.transpose(dkv, (1, 3, 0, 2)).reshape(KV_HEADS, 2 * head, tok)
    dk_t = dkv[:, :head].astype(jnp.float32)
    dq_t = from_lanes(dqt) * scale
    d_qkv_t = jnp.concatenate(
        [
            rotate_t(dq_t, cosine, -sine).astype(jnp.bfloat16).reshape(q_width, tok),
            rotate_t(dk_t, cosine, -sine).astype(jnp.bfloat16).reshape(kv_width, tok),
            dkv[:, head:].reshape(kv_width, tok),
        ],
        0,
    )
    grad_qkv = jnp.transpose(dot_nn(d_qkv_t, normed)).astype(jnp.bfloat16)
    d_norm_one = lax.dot_general(
        d_qkv_t, w_qkv, (((0,), (1,)), ((), ())), preferred_element_type=jnp.float32
    )
    d_input, grad_gain_one = norm_back(x_rows, gain_one, d_norm_one)
    grad_input = d_input + d_middle
    if by_halves:
        grad_wo, grad_qkv, grad_gain_one, grad_gain_two = reduce_rest(
            grad_wo, grad_qkv, grad_gain_one, grad_gain_two
        )
    else:
        grad_qkv, grad_gain_one, grad_gain_two = reduce_late(
            grad_qkv, grad_gain_one, grad_gain_two
        )
    return (
        arrange(result.astype(jnp.bfloat16))[None],
        arrange(grad_input)[None],
        grad_gain_one,
        grad_qkv[:, :q_width],
        grad_qkv[:, q_width : q_width + kv_width],
        grad_qkv[:, q_width + kv_width :],
        grad_wo,
        grad_gain_two,
        grad_ff[:, :ff],
        grad_ff[:, ff:],
        grad_wd,
    )


def reduce_early(grad_wd, grad_ff, grad_wo):
    def total(v):
        v = lax.psum_scatter(v, "fsdp", scatter_dimension=0, tiled=True)
        return lax.psum(v, "ctx").astype(jnp.float32)

    return total(grad_wd), total(grad_ff), total(grad_wo)


def reduce_late(grad_qkv, grad_gain_one, grad_gain_two):
    gains = jnp.stack([grad_gain_one, grad_gain_two], 1).astype(jnp.bfloat16)
    pack = jnp.concatenate([grad_qkv, gains], 1)
    pack = lax.psum_scatter(pack, "fsdp", scatter_dimension=0, tiled=True)
    pack = lax.psum(pack, "ctx").astype(jnp.float32)
    return pack[:, :-2], pack[:, -2], pack[:, -1]


def solution(mesh):
    placed = (
        P("fsdp", "ctx", None),
        P("fsdp", "ctx", None),
        P(),
        P("fsdp"),
        P("fsdp", None),
        P("fsdp", None),
        P("fsdp", None),
        P("fsdp", None),
        P("fsdp"),
        P("fsdp", None),
        P("fsdp", None),
        P("fsdp", None),
    )
    return jax.shard_map(
        body,
        mesh=mesh,
        in_specs=placed,
        out_specs=(
            P("fsdp", "ctx", None),
            P("fsdp", "ctx", None),
            P("fsdp"),
            P("fsdp", None),
            P("fsdp", None),
            P("fsdp", None),
            P("fsdp", None),
            P("fsdp"),
            P("fsdp", None),
            P("fsdp", None),
            P("fsdp", None),
        ),
        check_vma=False,
    )
```

```python
import functools

import jax
import jax.numpy as jnp
import numpy as np
from jax import lax
from jax.experimental import pallas as pl
from jax.experimental.pallas import tpu as pltpu
from jax.sharding import PartitionSpec as P

HEADS = 9
KV_HEADS = 3


eps_norm = 1e-05
rope_base = 100000.0


def rotate_t(v, cosine, sine):
    width = v.shape[-2] // 2
    first, second = (v[..., :width, :], v[..., width:, :])
    return jnp.concatenate([first * cosine - second * sine, second * cosine + first * sine], -2)


def normalize(v, gain):
    return v * lax.rsqrt(jnp.mean(v * v, -1, keepdims=True) + eps_norm) * gain


def norm_back(v, gain, grad):
    factor = lax.rsqrt(jnp.mean(v * v, -1, keepdims=True) + eps_norm)
    grad_gain = jnp.sum(grad * v * factor, 0)
    scaled = grad * gain
    grad_in = factor * scaled - v * factor**3 * jnp.mean(scaled * v, -1, keepdims=True)
    return (grad_in, grad_gain)


def inner(left, right):
    return lax.dot_general(
        left, right, (((0,), (0,)), ((), ())), preferred_element_type=jnp.float32
    )


def times_t(left, right):
    return lax.dot_general(
        left, right, (((1,), (1,)), ((), ())), preferred_element_type=jnp.float32
    )


def dot_tn(left, right):
    return lax.dot_general(
        left, right, (((0,), (0,)), ((), ())), preferred_element_type=jnp.float32
    )


def dot_nn(left, right):
    return jnp.dot(left, right, preferred_element_type=jnp.float32)


def causal(half, lanes, full):
    key = lax.broadcasted_iota(jnp.int32, (half, lanes), 0)
    lane = lax.broadcasted_iota(jnp.int32, (half, lanes), 1)
    return (key <= lax.rem(lane, half)) | (lane < full)


def over_blocks(place_ref, width, half, step):
    late, early = place_ref[0], place_ref[1]

    @pl.loop(0, early)
    def both(p):
        step(p, 2 * width, None)

    step(early, 2 * width, causal(half, 2 * width, width))

    @pl.loop(early + 1, late)
    def one(p):
        step(p, width, None)

    step(late, width, causal(half, width, 0))


def attend_kernel(stored_ref, place_ref, qt_ref, kv_ref, out_ref, lse_ref, top_ref, total_ref):
    kv_heads, head, lanes = out_ref.shape
    half = kv_ref.shape[2]
    top_ref[...] = jnp.full_like(top_ref, -1e30)
    total_ref[...] = jnp.zeros_like(total_ref)
    out_ref[...] = jnp.zeros_like(out_ref)

    def step(p, width, allowed):
        j = stored_ref[p]
        for g in range(kv_heads):
            kv = kv_ref[j, g]
            score = dot_nn(kv, qt_ref[g, :, :width])
            if allowed is not None:
                score = jnp.where(allowed, score, -1e30)
            top = top_ref[g, :, :width]
            new_top = jnp.maximum(top, jnp.max(score, 0, keepdims=True))
            weight = jnp.exp(score - new_top)
            fade = jnp.exp(top - new_top)
            top_ref[g, :, :width] = new_top
            total_ref[g, :, :width] = total_ref[g, :, :width] * fade + jnp.sum(
                weight, 0, keepdims=True
            )
            out_ref[g, :, :width] = (
                out_ref[g, :, :width] * fade + dot_tn(kv, weight.astype(jnp.bfloat16))[head:]
            )

    over_blocks(place_ref, lanes // 2, half, step)
    total = total_ref[...]
    lse_ref[...] = top_ref[...] + jnp.log(total)
    out_ref[...] = out_ref[...] / total


def attend_back_kernel(
    stored_ref, place_ref, qt_ref, qn_ref, dot_ref, don_ref, lse_ref, delta_ref, kv_ref,
    dq_ref, dkv_ref,
):
    kv_heads, head, lanes = dq_ref.shape
    half = kv_ref.shape[2]
    dq_ref[...] = jnp.zeros_like(dq_ref)

    def step(p, width, allowed):
        j = stored_ref[p]
        for g in range(kv_heads):
            kv = kv_ref[j, g]
            score = dot_nn(kv, qt_ref[g, :, :width])
            prob = jnp.exp(score - lse_ref[g, :, :width])
            if allowed is not None:
                prob = jnp.where(allowed, prob, 0.0)
            d_prob = dot_nn(kv, dot_ref[g, :, :width])
            d_score = (prob * (d_prob - delta_ref[g, :, :width])).astype(jnp.bfloat16)
            dkv_ref[j, g] = (
                dot_nn(d_score, qn_ref[g, :width]) + dot_nn(prob.astype(jnp.bfloat16), don_ref[g, :width])
            ).astype(jnp.bfloat16)
            dq_ref[g, :, :width] += dot_tn(kv, d_score)[:head]

    over_blocks(place_ref, lanes // 2, half, step)

    @pl.loop(place_ref[0] + 1, dkv_ref.shape[0])
    def unseen(p):
        dkv_ref[stored_ref[p]] = jnp.zeros(dkv_ref.shape[1:], dkv_ref.dtype)


def in_vmem(count):
    return [pl.BlockSpec(memory_space=pltpu.VMEM)] * count


def attend(stored, place, qt, kv):
    kv_heads, wide, lanes = qt.shape
    head = wide // 2
    work = kv.shape[0] * kv_heads * kv.shape[2] * lanes // 2
    return pl.pallas_call(
        attend_kernel,
        out_shape=(
            jax.ShapeDtypeStruct((kv_heads, head, lanes), jnp.float32),
            jax.ShapeDtypeStruct((kv_heads, 1, lanes), jnp.float32),
        ),
        in_specs=[pl.BlockSpec(memory_space=pltpu.SMEM)] * 2 + in_vmem(2),
        out_specs=tuple(in_vmem(2)),
        scratch_shapes=[pltpu.VMEM((kv_heads, 1, lanes), jnp.float32)] * 2,
        compiler_params=pltpu.CompilerParams(vmem_limit_bytes=48 << 20),
        cost_estimate=pl.CostEstimate(
            flops=4 * wide * work, bytes_accessed=2 * kv.size, transcendentals=work
        ),
        name="attend",
    )(stored, place, qt, kv)


def attend_back(stored, place, qt, qn, d_ot, d_on, lse, delta, kv):
    kv_heads, wide, lanes = qt.shape
    head = wide // 2
    work = kv.shape[0] * kv_heads * kv.shape[2] * lanes // 2
    return pl.pallas_call(
        attend_back_kernel,
        out_shape=(
            jax.ShapeDtypeStruct((kv_heads, head, lanes), jnp.float32),
            jax.ShapeDtypeStruct(kv.shape, jnp.bfloat16),
        ),
        in_specs=[pl.BlockSpec(memory_space=pltpu.SMEM)] * 2 + in_vmem(7),
        out_specs=tuple(in_vmem(2)),
        compiler_params=pltpu.CompilerParams(vmem_limit_bytes=48 << 20),
        cost_estimate=pl.CostEstimate(
            flops=10 * wide * work, bytes_accessed=4 * kv.size, transcendentals=work
        ),
        name="attend_back",
    )(stored, place, qt, qn, d_ot, d_on, lse, delta, kv)


def flip_bits(order):
    me, row = lax.axis_index("ctx"), lax.axis_index("fsdp")
    found = {}
    for name in order:
        if name == "y":
            found[name] = (row, {"fsdp": 1 - row})
        else:
            step = 1 << CTX_BITS.index(name)
            bit = lax.rem(lax.div(me, step), 2)
            found[name] = (bit, {"ctx": me + step - 2 * step * bit})
    return found


CTX_BITS = ("core", "x", "near", "far")


def at_axis(ref, axis, index):
    return ref.at[(slice(None),) * axis + (index,)]


def tiles(shape):
    return list(np.ndindex(*shape[:-2]))


def reduce_kernel(jobs, *refs):
    count = len(jobs)
    sources, outs = refs[:count], refs[count : 2 * count]
    rest = list(refs[2 * count :])
    landing = [[rest.pop(0) for _ in order] for _, order, _ in jobs]
    send, recv = rest
    bits = flip_bits([n for n in ("y",) + CTX_BITS if any(n in axes for axes, _, _ in jobs)])
    barrier = pltpu.get_barrier_semaphore()
    for _, partner in bits.values():
        pl.semaphore_signal(barrier, inc=1, device_id=partner, device_id_type=pl.DeviceIdType.MESH)
    pl.semaphore_wait(barrier, len(bits))
    used = 0

    def copy(src, dst, name):
        nonlocal used
        made = pltpu.make_async_remote_copy(
            src_ref=src,
            dst_ref=dst,
            send_sem=send.at[used],
            recv_sem=recv.at[used],
            device_id=bits[name][1],
            device_id_type=pl.DeviceIdType.MESH,
        )
        used += 1
        made.start()
        return made

    state = [[source, list(axes), None] for source, (axes, _, _) in zip(sources, jobs)]
    gathers = [list(reversed([n for n in order if n != "y"])) if g else [] for _, order, g in jobs]
    longest = max(len(order) + len(back) for (_, order, _), back in zip(jobs, gathers))

    def begin(i, stage):
        current, axes, _ = state[i]
        order = jobs[i][1]
        if stage < len(order):
            name = order[stage]
            k = axes.index(name)
            away = at_axis(current, k, 1 - bits[name][0])
            state[i][2] = copy(away, landing[i][stage], name)
        elif stage < len(order) + len(gathers[i]):
            name = gathers[i][stage - len(order)]
            done = gathers[i][: stage - len(order)]
            place = tuple(
                slice(None) if n in done else bits[n][0] for n in jobs[i][0] if n != "y"
            )
            part = outs[i].at[place]
            state[i][2] = copy(part, part, name)

    def finish(i, stage):
        current, axes, made = state[i]
        order = jobs[i][1]
        if stage < len(order):
            made.wait()
            name = order[stage]
            k = axes.index(name)
            got = landing[i][stage]
            last = stage == len(order) - 1
            for t in tiles(got.shape):
                mine = current[t[:k] + (bits[name][0],) + t[k:]]
                total = (mine.astype(jnp.float32) + got[t].astype(jnp.float32)).astype(got.dtype)
                if not last:
                    got[t] = total
                elif gathers[i]:
                    outs[i][tuple(bits[n][0] for n in jobs[i][0] if n != "y")] = total
                else:
                    outs[i][...] = total
            state[i][0], state[i][1] = got, axes[:k] + axes[k + 1 :]
        elif stage < len(order) + len(gathers[i]):
            made.wait()

    for i in range(count):
        begin(i, 0)
    for stage in range(longest):
        for i in range(count):
            finish(i, stage)
            begin(i, stage + 1)


def reduce_over(arrays, jobs, name, collective_id):
    outs, scratch, steps = [], [], 0
    for array, (axes, order, gather) in zip(arrays, jobs):
        tile = array.shape[-2:]
        lead = (2,) * (len(axes) - ("y" in axes)) if gather else ()
        outs.append(jax.ShapeDtypeStruct(lead + tile, array.dtype))
        scratch += [
            pltpu.VMEM((2,) * (len(axes) - 1 - s) + tile, array.dtype) for s in range(len(order))
        ]
        steps += len(order) + (len(order) - ("y" in axes) if gather else 0)
    return pl.pallas_call(
        functools.partial(reduce_kernel, jobs),
        out_shape=tuple(outs),
        in_specs=in_vmem(len(arrays)),
        out_specs=tuple(in_vmem(len(arrays))),
        scratch_shapes=scratch + [pltpu.SemaphoreType.DMA((steps,))] * 2,
        compiler_params=pltpu.CompilerParams(
            vmem_limit_bytes=52 << 20, collective_id=collective_id, has_side_effects=True
        ),
        cost_estimate=pl.CostEstimate(
            flops=sum(a.size for a in arrays),
            bytes_accessed=sum(4 * a.size for a in arrays),
            transcendentals=0,
        ),
        name=name,
    )(*arrays)


CTX_AXES = ("far", "near", "x", "core")


def reduce_main(dkv, grad_wd, grad_ff):
    bits = (2,) * 4
    width = grad_ff.shape[1]
    dkv_in = dkv.reshape(bits + (-1, dkv.shape[-1]))
    wd_in = grad_wd.reshape((2,) + bits + (-1, grad_wd.shape[1]))
    rows = grad_ff.shape[0] // 4
    ff_in = grad_ff.reshape(2, 2, rows, 8, width // 8)
    ff_in = jnp.transpose(ff_in, (0, 1, 3, 2, 4)).reshape((2,) + bits + (rows, width // 8))
    half = dkv_in.shape[-2] // 2
    jobs = (
        (CTX_AXES, ("core", "x", "near", "far"), False),
        (CTX_AXES, ("core", "near", "far", "x"), False),
        (("y",) + CTX_AXES, ("core", "y", "x", "near", "far"), True),
        (("y",) + CTX_AXES, ("core", "y", "near", "far", "x"), True),
    )
    one, two, ff, wd = reduce_over(
        (dkv_in[..., :half, :], dkv_in[..., half:, :], ff_in, wd_in), jobs, "reduce_main", 1
    )
    mine = jnp.concatenate([one, two], 0).reshape((2,) + dkv.shape[1:])
    ff = jnp.transpose(ff.reshape(2, 8, rows, width // 8), (0, 2, 1, 3)).reshape(2 * rows, width)
    return mine, ff.astype(jnp.float32), wd.reshape(-1, wd.shape[-1]).astype(jnp.float32)


def reduce_rest(grad_wo, grad_qkv, grad_gain_one, grad_gain_two):
    bits = (2,) * 4
    width = grad_wo.shape[1] + grad_qkv.shape[1]
    rows = grad_wo.shape[0] // 2
    block = -(-(rows + 2) // 64) * 16
    pack = jnp.concatenate([grad_wo, grad_qkv], 1).reshape(2, rows, width)
    gains = jnp.stack([grad_gain_one, grad_gain_two]).astype(pack.dtype).reshape(2, 2, rows)
    gains = jnp.pad(
        jnp.swapaxes(gains, 0, 1), ((0, 0), (0, 4 * block - rows - 2), (0, width - rows))
    )
    pack = jnp.concatenate([pack, gains], 1).reshape(2, 4, block, 4, width // 4)
    pack = jnp.transpose(pack, (0, 1, 3, 2, 4)).reshape((2,) + bits + (block, width // 4))
    jobs = ((("y",) + CTX_AXES, ("core", "y", "x", "near", "far"), True),)
    (pack,) = reduce_over((pack,), jobs, "reduce_rest", 2)
    pack = jnp.transpose(pack.reshape(4, 4, block, width // 4), (0, 2, 1, 3))
    pack = pack.reshape(4 * block, width).astype(jnp.float32)
    cut = grad_wo.shape[1]
    return pack[:rows, :cut], pack[:rows, cut:], pack[rows, :rows], pack[rows + 1, :rows]


def gather_kernel(spans, wide, *refs):
    count = len(spans)
    shards = refs[:count]
    refs = refs[count:]
    if wide:
        piece, refs = refs[0], refs[1:]
        everything, refs = refs[0], refs[1:]
    outs, (send, recv) = refs[:-2], refs[-2:]
    bits = flip_bits(("y", "core") + (("x", "near", "far") if wide else ()))
    barrier = pltpu.get_barrier_semaphore()
    for _, partner in bits.values():
        pl.semaphore_signal(barrier, inc=1, device_id=partner, device_id_type=pl.DeviceIdType.MESH)
    pl.semaphore_wait(barrier, len(bits))
    row, core = bits["y"][0], bits["core"][0]
    used = 0

    def copy(src, dst, name):
        nonlocal used
        made = pltpu.make_async_remote_copy(
            src_ref=src,
            dst_ref=dst,
            send_sem=send.at[used],
            recv_sem=recv.at[used],
            device_id=bits[name][1],
            device_id_type=pl.DeviceIdType.MESH,
        )
        used += 1
        made.start()
        return made

    if wide:
        mine = tuple(bits[n][0] for n in CTX_AXES)
        everything[mine] = piece[...]
        half = piece.shape[0] // 2
        orders = (("far", "near", "x", "core"), ("x", "far", "near", "core"))

        def spread(i, stage):
            done = orders[i][:stage]
            at = tuple(slice(None) if n in done else bits[n][0] for n in CTX_AXES)
            part = everything.at[at + (pl.ds(i * half, half),)]
            return copy(part, part, orders[i][stage])

        moving = [spread(i, 0) for i in range(2)]

    def place(i, first, second):
        out, column = spans[i]
        height, width = shards[i].shape[0] // 2, shards[i].shape[1]
        return outs[out].at[first, second, :, pl.ds(column, width)], height

    over_y = []
    for i in range(count):
        target, height = place(i, row, core)
        part = shards[i].at[pl.ds(pl.multiple_of(core * height, 16), height)]
        over_y.append(copy(part, target, "y"))
    for i in range(count):
        for h in range(2):
            target, height = place(i, row, h)
            target[...] = shards[i][h * height : (h + 1) * height]
    if wide:
        for stage in range(1, 4):
            for i in range(2):
                moving[i].wait()
                moving[i] = spread(i, stage)
    over_core = []
    for i in range(count):
        over_y[i].wait()
        target, _ = place(i, 1 - row, core)
        over_core.append(copy(target, target, "core"))
    for made in over_core + (moving if wide else []):
        made.wait()


def gather_over(shards, spans, piece, name, collective_id):
    wide = piece is not None
    widths = {}
    for shard, (out, column) in zip(shards, spans):
        widths[out] = (shard.shape[0] // 2, max(widths.get(out, (0, 0))[1], column + shard.shape[1]))
    outs = [jax.ShapeDtypeStruct((2, 2) + widths[out], jnp.bfloat16) for out in sorted(widths)]
    operands = list(shards)
    if wide:
        operands.append(piece)
        outs.insert(0, jax.ShapeDtypeStruct((2,) * 4 + piece.shape, piece.dtype))
    steps = 2 * len(shards) + (8 if wide else 0)
    found = pl.pallas_call(
        functools.partial(gather_kernel, spans, wide),
        out_shape=tuple(outs),
        in_specs=in_vmem(len(operands)),
        out_specs=tuple(in_vmem(len(outs))),
        scratch_shapes=[pltpu.SemaphoreType.DMA((steps,))] * 2,
        compiler_params=pltpu.CompilerParams(
            vmem_limit_bytes=48 << 20, collective_id=collective_id, has_side_effects=True
        ),
        name=name,
    )(*operands)
    weights = [v.reshape(-1, v.shape[-1]) for v in found[1 if wide else 0 :]]
    return ([found[0]] if wide else []) + weights


def body(
    tokens,
    cotangent,
    block_place,
    norm_attn,
    w_query,
    w_key,
    w_value,
    w_out,
    norm_ffn,
    w_gate,
    w_up,
    w_down,
):
    here = lax.axis_index("ctx")
    tok = tokens.shape[1]
    half = tok // 2
    blocks = block_place.shape[0]
    groups = HEADS // KV_HEADS
    head = w_query.shape[1] // HEADS
    q_width = HEADS * head
    kv_width = KV_HEADS * head
    scale = head ** (-0.5)
    ff = w_gate.shape[1]

    mine = lax.dynamic_slice_in_dim(block_place, 2 * here, 2)
    swap = mine[0] < mine[1]
    place = jnp.where(swap, mine[::-1], mine)
    order = jnp.arange(blocks, dtype=jnp.int32)
    at = jnp.sum(jnp.where(block_place[None, :] == order[:, None], order[None, :], 0), 1)
    stored = (at // 2 * 2 + (order < blocks // 2)).astype(jnp.int32)

    def arrange(rows):
        return jnp.where(swap, jnp.concatenate([rows[half:], rows[:half]], 0), rows)

    first_pack = jnp.concatenate(
        [w_query, w_key, w_value, norm_attn[:, None], norm_ffn[:, None]], 1
    )
    by_halves = lax.axis_size("ctx") == 16 and lax.axis_size("fsdp") == 2
    if by_halves:
        (first_pack,) = gather_over((first_pack,), ((0, 0),), None, "gather_first", 3)
    else:
        first_pack = lax.all_gather(first_pack, "fsdp", axis=0, tiled=True)
    w_qkv = first_pack[:, : q_width + 2 * kv_width]
    gain_one = first_pack[:, -2].astype(jnp.float32)
    gain_two = first_pack[:, -1].astype(jnp.float32)

    x_rows = arrange(tokens[0]).astype(jnp.float32)
    seed_grad = arrange(cotangent[0])
    positions = (place[:, None] * half + jnp.arange(half, dtype=jnp.int32)[None, :]).reshape(tok)
    freq = rope_base ** (-2.0 * jnp.arange(head // 2, dtype=jnp.float32) / head)
    angle = freq[:, None] * positions.astype(jnp.float32)[None, :]
    cosine, sine = jnp.cos(angle), jnp.sin(angle)

    normed = normalize(x_rows, gain_one).astype(jnp.bfloat16)
    qkv_t = lax.dot_general(
        w_qkv, normed, (((0,), (1,)), ((), ())), preferred_element_type=jnp.float32
    )
    query = rotate_t(qkv_t[:q_width].reshape(HEADS, head, tok), cosine, sine).astype(jnp.bfloat16)
    keys = rotate_t(
        qkv_t[q_width : q_width + kv_width].reshape(KV_HEADS, head, tok), cosine, sine
    ).astype(jnp.bfloat16)
    values = qkv_t[q_width + kv_width :].reshape(KV_HEADS, head, tok).astype(jnp.bfloat16)
    kv = jnp.concatenate([keys, values], 1).reshape(KV_HEADS, 2 * head, 2, half)
    kv = jnp.transpose(kv, (2, 0, 3, 1))
    if by_halves:
        kv, wo, w_ff, wd = gather_over(
            (w_out, w_gate, w_up, w_down),
            ((0, 0), (1, 0), (1, ff), (2, 0)),
            kv.reshape(-1, 2 * head),
            "gather_rest",
            4,
        )
        kv = kv.reshape(blocks, KV_HEADS, half, 2 * head)
    else:
        kv = lax.all_gather(kv, "ctx", axis=0, tiled=True)
        wo = lax.all_gather(w_out, "fsdp", axis=0, tiled=True)
        w_ff = lax.all_gather(jnp.concatenate([w_gate, w_up], 1), "fsdp", axis=0, tiled=True)
        wd = lax.all_gather(w_down, "fsdp", axis=0, tiled=True)

    def to_lanes(v):
        v = v.reshape(KV_HEADS, groups, head, 2, half)
        return jnp.transpose(v, (0, 2, 3, 1, 4)).reshape(KV_HEADS, head, 2 * groups * half)

    def from_lanes(v):
        v = v.reshape(KV_HEADS, head, 2, groups, half)
        return jnp.transpose(v, (0, 3, 1, 2, 4)).reshape(HEADS, head, tok)

    qt = to_lanes(query * jnp.bfloat16(scale))
    qt = jnp.concatenate([qt, jnp.zeros_like(qt)], 1)
    qn = jnp.swapaxes(qt, 1, 2)
    attn, lse = attend(stored, place, qt, kv)

    mixed = jnp.transpose(from_lanes(attn.astype(jnp.bfloat16)).reshape(q_width, tok))
    middle = x_rows + dot_nn(mixed, wo)
    normed_two = normalize(middle, gain_two).astype(jnp.bfloat16)
    gate_up = dot_nn(normed_two, w_ff)
    gate, upper = gate_up[:, :ff], gate_up[:, ff:]
    sig = jax.nn.sigmoid(gate)
    hidden = (gate * sig * upper).astype(jnp.bfloat16)
    result = middle + dot_nn(hidden, wd)
    d_hidden = times_t(seed_grad, wd)
    grad_wd = inner(hidden, seed_grad).astype(jnp.bfloat16)
    d_gate = (d_hidden * upper * sig * (1.0 + gate * (1.0 - sig))).astype(jnp.bfloat16)
    d_up = (d_hidden * gate * sig).astype(jnp.bfloat16)
    d_ff = jnp.concatenate([d_gate, d_up], 1)
    grad_ff = inner(normed_two, d_ff).astype(jnp.bfloat16)
    d_norm_two = times_t(d_ff, w_ff)
    d_middle, grad_gain_two = norm_back(middle, gain_two, d_norm_two)
    d_middle = d_middle + seed_grad.astype(jnp.float32)
    d_branch = d_middle.astype(jnp.bfloat16)
    grad_wo = inner(mixed, d_branch).astype(jnp.bfloat16)
    d_mixed_t = times_t(wo, d_branch).astype(jnp.bfloat16)
    d_ot = to_lanes(d_mixed_t)
    delta = jnp.sum(d_ot.astype(jnp.float32) * attn, 1, keepdims=True)
    d_ot = jnp.concatenate([jnp.zeros_like(d_ot), d_ot], 1)
    d_on = jnp.swapaxes(d_ot, 1, 2)

    dqt, dkv = attend_back(stored, place, qt, qn, d_ot, d_on, lse, delta, kv)
    if by_halves:
        dkv, grad_ff, grad_wd = reduce_main(dkv, grad_wd, grad_ff)
    else:
        grad_wd, grad_ff, grad_wo = reduce_early(grad_wd, grad_ff, grad_wo)
        dkv = lax.psum_scatter(dkv, "ctx", scatter_dimension=0, tiled=True)
    dkv = jnp.transpose(dkv, (1, 3, 0, 2)).reshape(KV_HEADS, 2 * head, tok)
    dk_t = dkv[:, :head].astype(jnp.float32)
    dq_t = from_lanes(dqt) * scale
    d_qkv_t = jnp.concatenate(
        [
            rotate_t(dq_t, cosine, -sine).astype(jnp.bfloat16).reshape(q_width, tok),
            rotate_t(dk_t, cosine, -sine).astype(jnp.bfloat16).reshape(kv_width, tok),
            dkv[:, head:].reshape(kv_width, tok),
        ],
        0,
    )
    grad_qkv = jnp.transpose(dot_nn(d_qkv_t, normed)).astype(jnp.bfloat16)
    d_norm_one = lax.dot_general(
        d_qkv_t, w_qkv, (((0,), (1,)), ((), ())), preferred_element_type=jnp.float32
    )
    d_input, grad_gain_one = norm_back(x_rows, gain_one, d_norm_one)
    grad_input = d_input + d_middle
    if by_halves:
        grad_wo, grad_qkv, grad_gain_one, grad_gain_two = reduce_rest(
            grad_wo, grad_qkv, grad_gain_one, grad_gain_two
        )
    else:
        grad_qkv, grad_gain_one, grad_gain_two = reduce_late(
            grad_qkv, grad_gain_one, grad_gain_two
        )
    return (
        arrange(result.astype(jnp.bfloat16))[None],
        arrange(grad_input)[None],
        grad_gain_one,
        grad_qkv[:, :q_width],
        grad_qkv[:, q_width : q_width + kv_width],
        grad_qkv[:, q_width + kv_width :],
        grad_wo,
        grad_gain_two,
        grad_ff[:, :ff],
        grad_ff[:, ff:],
        grad_wd,
    )


def reduce_early(grad_wd, grad_ff, grad_wo):
    def total(v):
        v = lax.psum_scatter(v, "fsdp", scatter_dimension=0, tiled=True)
        return lax.psum(v, "ctx").astype(jnp.float32)

    return total(grad_wd), total(grad_ff), total(grad_wo)


def reduce_late(grad_qkv, grad_gain_one, grad_gain_two):
    gains = jnp.stack([grad_gain_one, grad_gain_two], 1).astype(jnp.bfloat16)
    pack = jnp.concatenate([grad_qkv, gains], 1)
    pack = lax.psum_scatter(pack, "fsdp", scatter_dimension=0, tiled=True)
    pack = lax.psum(pack, "ctx").astype(jnp.float32)
    return pack[:, :-2], pack[:, -2], pack[:, -1]


def solution(mesh):
    placed = (
        P("fsdp", "ctx", None),
        P("fsdp", "ctx", None),
        P(),
        P("fsdp"),
        P("fsdp", None),
        P("fsdp", None),
        P("fsdp", None),
        P("fsdp", None),
        P("fsdp"),
        P("fsdp", None),
        P("fsdp", None),
        P("fsdp", None),
    )
    return jax.shard_map(
        body,
        mesh=mesh,
        in_specs=placed,
        out_specs=(
            P("fsdp", "ctx", None),
            P("fsdp", "ctx", None),
            P("fsdp"),
            P("fsdp", None),
            P("fsdp", None),
            P("fsdp", None),
            P("fsdp", None),
            P("fsdp"),
            P("fsdp", None),
            P("fsdp", None),
            P("fsdp", None),
        ),
        check_vma=False,
    )
```
